32 devices in a mesh: row: 4 (over y, x), col: 8 (over z, core).
Axes of the slice: x: 2, y: 2, z: 4, core: 2. Of those that a mesh axis runs over, the one named last changes fastest.
Arguments:
- inputs: bfloat16 [4096, 4096], P('row', 'col'), may hold values from -5 to 5
- norm_gain: float32 [4096], replicated, may hold values from 0.25 to 1.75
- query_train: float32 [4096, 4096], P(('row', 'col')), as said below
- key_train: float32 [4096, 4096], P(('row', 'col')), as said below
- value_train: float32 [4096, 4096], P(('row', 'col')), may hold values from -0.09375 to 0.09375
- out_train: float32 [4096, 2048], P(None, ('row', 'col')), may hold values from -0.09375 to 0.09375
- adapter_down: bfloat16 [4096, 128], replicated, may hold values from -0.09375 to 0.09375
- adapter_up: bfloat16 [128, 3, 32, 128], P(None, None, 'col'), may hold values from -0.5 to 0.5
- lengths: int32 [4, 7], P('row'), may hold values from 1 to 512, 1024 in all within a row
Outputs:
- mixed: bfloat16 [4096, 2048], P(('row', 'col'))
The draws below stay inside these ranges and needn't reach their ends.
Inputs may be any that keep to these rules, and one draw needn't show every extreme that they name: In each token group the 7 lengths sum to 1024; the longest is 512. `query_train`: entries are of order 1 / sqrt(4096) and at most 32 / sqrt(4096) in magnitude. `key_train`: entries are of order 1 / sqrt(4096) and at most 32 / sqrt(4096) in magnitude.
All inputs are finite; a program needn't handle non-finite values.
Results may differ from the reference program's by a relative error of at most 0.018.
Values may be sent and summed in bfloat16 or wider, within the bound.
A program may use at most 128 MiB of HBM per device.

```python
import math
import jax
import jax.numpy as jnp
import numpy as np
from jax import lax

DIN = 4096
HEADS = 32
HS = 128
DOUT = 2048
RANK = 128
TOK_ROW = 1024
PROMPTS = 7
MOST = 512
GROUPS = 4
TOKENS = 4096


def own_matrix(key, label):
    own_part = jnp.clip(jax.random.normal(jax.random.fold_in(key, label), (DIN, HEADS, HS), jnp.float32), -6.0, 6.0)
    return own_part / math.sqrt(DIN)


def draw_query_train(key, part):
    result = own_matrix(key, 21)
    return result.reshape(DIN, HEADS * HS).astype(jnp.float32)


def draw_key_train(key, part):
    result = own_matrix(key, 22)
    return result.reshape(DIN, HEADS * HS).astype(jnp.float32)


def draw_inputs(key, part):
    result = jnp.clip(jax.random.normal(jax.random.fold_in(key, 34), (TOKENS, DIN), jnp.float32), -5.0, 5.0)
    return result.astype(jnp.bfloat16)


def block_scale(own_key, dims, cuts, least, high):
    level = 1.0
    for dim, shards_of in cuts:
        heights = jax.random.uniform(jax.random.fold_in(jax.random.fold_in(own_key, 6), dim), (shards_of,), jnp.float32, least / len(cuts), high / len(cuts))
        level = level * jnp.repeat(jnp.exp(heights), dims[dim] // shards_of).reshape((-1,) + (1,) * (len(dims) - 1 - dim))
    return level


def profile(amount, total, limit, lean):
    loads = [(1 << 20) // math.isqrt(grade ** lean) + 1 for grade in range(2, amount + 1)]
    surplus, counts = total - limit - (amount - 1), [1] * (amount - 1)
    while surplus > 0:
        free = [i for i in range(amount - 1) if counts[i] < limit]
        mass, left = sum([loads[i] for i in free]), surplus
        for i in free:
            more = min(limit - counts[i], max(1, left * loads[i] // mass), surplus)
            counts[i] = counts[i] + more
            surplus = surplus - more
    return np.array([limit] + counts)


def uneven_parts(rng, number_of, total, reach, skew):
    if number_of == 2:
        one = jax.random.randint(rng, (), max(1, total - reach), min(reach, total - 1) + 1)
        return jnp.stack([one, total - one])
    sizes = jnp.asarray(profile(number_of, total, reach, skew), jnp.int32)
    couples = (number_of - 1) // 2
    giver, taker = sizes[1:1 + 2 * couples:2], sizes[2:2 + 2 * couples:2]
    margin = jnp.minimum(giver - 1, reach - taker)
    passed = jax.random.randint(jax.random.fold_in(rng, 1), (couples,), 0, 1 << 20) % (margin + 1)
    sizes = sizes.at[1:1 + 2 * couples:2].set(giver - passed).at[2:2 + 2 * couples:2].set(taker + passed)
    return sizes[jax.random.permutation(jax.random.fold_in(rng, 2), number_of)]


def scatter_about(own_key, extent, deviation, most, split=(), kind=jnp.bfloat16):
    values = jax.random.normal(own_key, extent, jnp.float32) * deviation
    if len(split) > 0:
        values = block_scale(own_key, extent, split, -0.22, 0.18) * values
    return jnp.clip(values, min=-most, max=most).astype(kind)


def setup_inputs(seed: int = 0) -> dict:
    splits = jax.random.split(jax.random.key(seed), 10)
    return {
        "inputs": draw_inputs(jax.random.fold_in(splits[9], 71), 0),
        "norm_gain": jnp.clip(1.0 + 0.15 * jax.random.normal(splits[1], (DIN,), jnp.float32), 0.25, 1.75),
        "query_train": draw_query_train(jax.random.fold_in(splits[9], 71), 0),
        "key_train": draw_key_train(jax.random.fold_in(splits[9], 71), 0),
        "value_train": scatter_about(splits[4], (DIN, HEADS * HS), DIN ** -0.5, 0.09375, ((0, 32),), jnp.float32),
        "out_train": scatter_about(splits[5], (HEADS * HS, DOUT), (HEADS * HS) ** -0.5, 0.09375, ((1, 32),), jnp.float32),
        "adapter_down": scatter_about(splits[6], (DIN, RANK), DIN ** -0.5, 0.09375),
        "adapter_up": scatter_about(splits[7], (RANK, 3, HEADS, HS), RANK ** -0.5, 0.5, ((2, 8),)),
        "lengths": jax.vmap(lambda own: uneven_parts(own, PROMPTS, TOK_ROW, MOST, 2))(jax.random.split(splits[8], GROUPS)).reshape((GROUPS, PROMPTS)).astype(jnp.int32),
    }


def normalize(inputs, norm_gain):
    floats = inputs.astype(jnp.float32)
    mean_square = lax.optimization_barrier(jnp.mean(floats * floats, axis=1, keepdims=True))
    return (floats * lax.rsqrt(mean_square + 1e-05) * norm_gain).astype(jnp.bfloat16)

def segment_of(lengths_row, tok_count):
    position = jnp.arange(tok_count, dtype=jnp.int32)
    prompt_ends = jnp.cumsum(lengths_row.astype(jnp.int32))
    return lax.optimization_barrier(jnp.sum((position[:, None] >= prompt_ends[None, :]).astype(jnp.int32), axis=1))

def attend(queries, keys_all, values_all, segment):
    tok_count = queries.shape[0]
    block_rows = min(512, tok_count)
    factor = 1.0 / math.sqrt(queries.shape[2])
    key_pos = jnp.arange(tok_count, dtype=jnp.int32)
    keys_wide = keys_all.astype(jnp.float32)
    values_wide = values_all.astype(jnp.float32)

    def one_block(first):
        query_blk = lax.dynamic_slice_in_dim(queries, first, block_rows, 0).astype(jnp.float32)
        query_pos = first + jnp.arange(block_rows, dtype=jnp.int32)
        query_seg = lax.dynamic_slice_in_dim(segment, first, block_rows, 0)
        scores = jnp.einsum('qhd,khd->hqk', query_blk, keys_wide) * factor
        allowed = (query_seg[:, None] == segment[None, :]) & (key_pos[None, :] <= query_pos[:, None])
        scores = jnp.where(allowed[None], scores, -1e+30)
        highest = lax.optimization_barrier(jnp.max(scores, axis=2, keepdims=True))
        exponent = jnp.exp(scores - highest)
        weights = (exponent / lax.optimization_barrier(jnp.sum(exponent, axis=2, keepdims=True))).astype(jnp.bfloat16)
        return jnp.einsum('hqk,khd->qhd', weights.astype(jnp.float32), values_wide).astype(jnp.bfloat16)
    starts = jnp.arange(tok_count // block_rows, dtype=jnp.int32) * block_rows
    blocks = lax.map(one_block, starts)
    return blocks.reshape(tok_count, queries.shape[1] * queries.shape[2])

def reference(inputs, norm_gain, query_train, key_train, value_train, out_train, adapter_down, adapter_up, lengths):
    normed = normalize(inputs, norm_gain)
    adapted = jnp.dot(normed, adapter_down, preferred_element_type=jnp.float32).astype(jnp.bfloat16)
    projected = []
    for part_idx, trained in enumerate((query_train, key_train, value_train)):
        product = jnp.dot(normed, trained.astype(jnp.bfloat16), preferred_element_type=jnp.float32)
        adapter_term = jnp.dot(adapted, adapter_up[:, part_idx].reshape(RANK, HEADS * HS), preferred_element_type=jnp.float32)
        projected.append((product + adapter_term).astype(jnp.bfloat16).reshape(TOKENS, HEADS, HS))
    results = []
    for group_idx in range(GROUPS):
        first_row = group_idx * TOK_ROW
        segment = segment_of(lengths[group_idx], TOK_ROW)
        results.append(attend(projected[0][first_row:first_row + TOK_ROW], projected[1][first_row:first_row + TOK_ROW], projected[2][first_row:first_row + TOK_ROW], segment))
    attended = jnp.concatenate(results, axis=0)
    return jnp.dot(attended, out_train.astype(jnp.bfloat16), preferred_element_type=jnp.float32).astype(jnp.bfloat16)
```

```python
import math

import jax
import jax.numpy as jnp
from jax import lax
from jax.sharding import PartitionSpec as P

HEADS = 32
HS = 128


def normalize(whole, norm_gain):
    floats = whole.astype(jnp.float32)
    mean_square = jnp.mean(floats * floats, axis=1, keepdims=True)
    return (floats * lax.rsqrt(mean_square + 1e-05) * norm_gain).astype(jnp.bfloat16)


def segment_of(lengths_row, tok_count):
    position = jnp.arange(tok_count, dtype=jnp.int32)
    order = jnp.arange(lengths_row.shape[0], dtype=jnp.int32)
    prompt_ends = jnp.sum(
        jnp.where(order[:, None] <= order[None, :], lengths_row[:, None], 0), axis=0
    )
    return jnp.sum((position[:, None] >= prompt_ends[None, :]).astype(jnp.int32), axis=1)


def attend(queries, keys_all, values_all, segment):
    tok_count = queries.shape[0]
    block_rows = min(512, tok_count)
    factor = 1.0 / math.sqrt(queries.shape[2])
    key_pos = jnp.arange(tok_count, dtype=jnp.int32)

    def one_block(first):
        query_blk = lax.dynamic_slice_in_dim(queries, first, block_rows, 0)
        query_pos = first + jnp.arange(block_rows, dtype=jnp.int32)
        query_seg = lax.dynamic_slice_in_dim(segment, first, block_rows, 0)
        scores = (
            jnp.einsum("qhd,khd->hqk", query_blk, keys_all, preferred_element_type=jnp.float32)
            * factor
        )
        allowed = (query_seg[:, None] == segment[None, :]) & (
            key_pos[None, :] <= query_pos[:, None]
        )
        scores = jnp.where(allowed[None], scores, -1e30)
        highest = jnp.max(scores, axis=2, keepdims=True)
        exponent = jnp.exp(scores - highest)
        weights = (exponent / jnp.sum(exponent, axis=2, keepdims=True)).astype(jnp.bfloat16)
        return jnp.einsum(
            "hqk,khd->qhd", weights, values_all, preferred_element_type=jnp.float32
        ).astype(jnp.bfloat16)

    starts = jnp.arange(tok_count // block_rows, dtype=jnp.int32) * block_rows
    blocks = lax.map(one_block, starts)
    return blocks.reshape(tok_count, queries.shape[1] * queries.shape[2])


def on_device(
    inputs,
    norm_gain,
    query_train,
    key_train,
    value_train,
    out_train,
    adapter_down,
    adapter_up,
    lengths,
):
    col_count = lax.axis_size("col")
    whole = lax.all_gather(inputs, "col", axis=1, tiled=True)
    normed = normalize(whole, norm_gain)
    tok_count = normed.shape[0]
    adapted = jnp.dot(normed, adapter_down, preferred_element_type=jnp.float32).astype(jnp.bfloat16)
    local_rows = query_train.shape[0]
    head_local = HEADS // col_count
    merged_width = 3 * head_local * HS
    query_half = query_train.astype(jnp.bfloat16).reshape(local_rows, HEADS, HS)
    key_half = key_train.astype(jnp.bfloat16).reshape(local_rows, HEADS, HS)
    value_half = value_train.astype(jnp.bfloat16).reshape(local_rows, HEADS, HS)
    moved = (
        lax.all_to_all(query_half, "col", split_axis=1, concat_axis=0, tiled=True),
        lax.all_to_all(key_half, "col", split_axis=1, concat_axis=0, tiled=True),
        lax.all_to_all(value_half, "col", split_axis=1, concat_axis=0, tiled=True),
    )
    merged = jnp.stack(moved, axis=1).reshape(moved[0].shape[0], merged_width)
    product = jnp.dot(
        normed,
        lax.all_gather(merged, "row", axis=0, tiled=True),
        preferred_element_type=jnp.float32,
    )
    up_columns = adapter_up.reshape(adapter_up.shape[0], merged_width)
    joined = (product + jnp.dot(adapted, up_columns, preferred_element_type=jnp.float32)).astype(
        jnp.bfloat16
    )
    joined = joined.reshape(tok_count, 3, head_local, HS)
    segment = segment_of(lengths[0], tok_count)
    attended = attend(joined[:, 0], joined[:, 1], joined[:, 2], segment)
    out_local = out_train.astype(jnp.bfloat16)
    out_block = lax.all_to_all(out_local, "col", split_axis=0, concat_axis=1, tiled=True)
    partial_out = jnp.dot(
        attended,
        lax.all_gather(out_block, "row", axis=1, tiled=True),
        preferred_element_type=jnp.float32,
    )
    mixed = lax.psum_scatter(
        partial_out.astype(jnp.bfloat16), "col", scatter_dimension=0, tiled=True
    )
    return mixed


def solution(mesh):
    in_specs = (
        P("row", "col"),
        P(),
        P(("row", "col"), None),
        P(("row", "col"), None),
        P(("row", "col"), None),
        P(None, ("row", "col")),
        P(),
        P(None, None, "col", None),
        P("row", None),
    )
    out_specs = P(("row", "col"), None)
    return jax.shard_map(
        on_device, mesh=mesh, in_specs=in_specs, out_specs=out_specs, check_vma=False
    )
```

```python
import math

import jax
import jax.numpy as jnp
from jax import lax
from jax.sharding import PartitionSpec as P

HEADS = 32
HS = 128
MOST = 512


def segment_of(lengths_row, tok_count):
    position = jnp.arange(tok_count, dtype=jnp.int32)
    order = jnp.arange(lengths_row.shape[0], dtype=jnp.int32)
    prompt_ends = jnp.sum(
        jnp.where(order[:, None] <= order[None, :], lengths_row[:, None], 0), axis=0
    )
    return jnp.sum((position[:, None] >= prompt_ends[None, :]).astype(jnp.int32), axis=1)


def attend(queries, keys_all, values_all, segment, heads):
    tok_count = queries.shape[0]
    block = min(256, tok_count)
    factor = 1.0 / math.sqrt(HS)
    out = []
    for head in range(heads):
        lanes = slice(head * HS, (head + 1) * HS)
        rows = []
        for first in range(0, tok_count, block):
            low = max(0, (first - MOST + 1) // block * block)
            end = first + block
            scores = (
                lax.dot_general(
                    queries[first:end, lanes],
                    keys_all[low:end, lanes],
                    (((1,), (1,)), ((), ())),
                    preferred_element_type=jnp.float32,
                )
                * factor
            )
            query_pos = first + jnp.arange(block, dtype=jnp.int32)
            key_pos = low + jnp.arange(end - low, dtype=jnp.int32)
            allowed = (segment[first:end, None] == segment[None, low:end]) & (
                key_pos[None, :] <= query_pos[:, None]
            )
            scores = jnp.where(allowed, scores, -1e30)
            highest = jnp.max(scores, axis=1, keepdims=True)
            exponent = jnp.exp(scores - highest)
            weights = (exponent / jnp.sum(exponent, axis=1, keepdims=True)).astype(jnp.bfloat16)
            rows.append(
                jnp.dot(
                    weights, values_all[low:end, lanes], preferred_element_type=jnp.float32
                ).astype(jnp.bfloat16)
            )
        out.append(jnp.concatenate(rows, axis=0))
    return jnp.concatenate(out, axis=1)


def on_device(
    inputs,
    norm_gain,
    query_train,
    key_train,
    value_train,
    out_train,
    adapter_down,
    adapter_up,
    lengths,
):
    cols = lax.axis_size("col")
    rows, features = query_train.shape
    heads = HEADS // cols
    width = heads * HS

    def serve(trained):
        half = trained.astype(jnp.bfloat16).reshape(rows, cols, width).transpose(1, 0, 2)
        moved = lax.all_to_all(half, "col", split_axis=0, concat_axis=0)
        return moved.reshape(cols * rows, width)

    parts = []
    for trained in (query_train, key_train, value_train):
        parts.append(lax.all_gather(serve(trained), "row", axis=0, tiled=True))
    whole = lax.all_gather(inputs, "col", axis=1, tiled=True)
    out_half = out_train.astype(jnp.bfloat16).T
    out_half = out_half.reshape(out_half.shape[0], cols, width).transpose(1, 0, 2)
    out_moved = lax.all_to_all(out_half, "col", split_axis=0, concat_axis=0)
    out_t = lax.all_gather(out_moved.reshape(-1, width), "row", axis=0, tiled=True)

    floats = whole.astype(jnp.float32)
    mean_square = jnp.mean(floats * floats, axis=1, keepdims=True)
    normed = (floats * lax.rsqrt(mean_square + 1e-05) * norm_gain).astype(jnp.bfloat16)
    adapted = jnp.dot(normed, adapter_down, preferred_element_type=jnp.float32).astype(jnp.bfloat16)
    projected = []
    for s in range(3):
        up = adapter_up[:, s].reshape(adapter_up.shape[0], width)
        projected.append(
            (
                jnp.dot(normed, parts[s], preferred_element_type=jnp.float32)
                + jnp.dot(adapted, up, preferred_element_type=jnp.float32)
            ).astype(jnp.bfloat16)
        )
    segment = segment_of(lengths[0], normed.shape[0])
    attended = attend(*projected, segment, heads)
    partial_out = lax.dot_general(
        attended, out_t, (((1,), (1,)), ((), ())), preferred_element_type=jnp.float32
    )
    return lax.psum_scatter(
        partial_out.astype(jnp.bfloat16), "col", scatter_dimension=0, tiled=True
    )


def solution(mesh):
    in_specs = (
        P("row", "col"),
        P(),
        P(("row", "col"), None),
        P(("row", "col"), None),
        P(("row", "col"), None),
        P(None, ("row", "col")),
        P(),
        P(None, None, "col", None),
        P("row", None),
    )
    out_specs = P(("row", "col"), None)
    return jax.shard_map(
        on_device, mesh=mesh, in_specs=in_specs, out_specs=out_specs, check_vma=False
    )
```

```python
import functools
import math

import jax
import jax.numpy as jnp
from jax import lax
from jax.experimental import pallas as pl
from jax.experimental.pallas import tpu as pltpu
from jax.sharding import PartitionSpec as P

HEADS = 32
HS = 128
MOST = 512


def segment_of(lengths_row, tok_count):
    position = jnp.arange(tok_count, dtype=jnp.int32)
    order = jnp.arange(lengths_row.shape[0], dtype=jnp.int32)
    prompt_ends = jnp.sum(
        jnp.where(order[:, None] <= order[None, :], lengths_row[:, None], 0), axis=0
    )
    return jnp.sum((position[:, None] >= prompt_ends[None, :]).astype(jnp.int32), axis=1)


def attend(queries, keys_all, values_all, segment, heads):
    tok_count = queries.shape[0]
    block = min(256, tok_count)
    factor = 1.0 / math.sqrt(HS)
    out = []
    for head in range(heads):
        lanes = slice(head * HS, (head + 1) * HS)
        rows = []
        for first in range(0, tok_count, block):
            low = max(0, (first - MOST + 1) // block * block)
            end = first + block
            scores = (
                lax.dot_general(
                    queries[first:end, lanes],
                    keys_all[low:end, lanes],
                    (((1,), (1,)), ((), ())),
                    preferred_element_type=jnp.float32,
                )
                * factor
            )
            query_pos = first + jnp.arange(block, dtype=jnp.int32)
            key_pos = low + jnp.arange(end - low, dtype=jnp.int32)
            allowed = (segment[first:end, None] == segment[None, low:end]) & (
                key_pos[None, :] <= query_pos[:, None]
            )
            scores = jnp.where(allowed, scores, -1e30)
            highest = jnp.max(scores, axis=1, keepdims=True)
            exponent = jnp.exp(scores - highest)
            weights = (exponent / jnp.sum(exponent, axis=1, keepdims=True)).astype(jnp.bfloat16)
            rows.append(
                jnp.dot(
                    weights, values_all[low:end, lanes], preferred_element_type=jnp.float32
                ).astype(jnp.bfloat16)
            )
        out.append(jnp.concatenate(rows, axis=0))
    return jnp.concatenate(out, axis=1)


def move_kernel(
    row_n,
    col_n,
    x,
    w0,
    w1,
    w2,
    w3,
    whole,
    d0,
    d1,
    d2,
    d3,
    local_sem,
    a_send,
    a_recv,
    r_send,
    r_recv,
    g_send,
    g_recv,
    c_send,
    c_recv,
    s_send,
    s_recv,
):
    src, dst = (w0, w1, w2, w3), (d0, d1, d2, d3)
    r, c = lax.axis_index("row"), lax.axis_index("col")
    chain = col_n // 2
    place, core = c // 2, c % 2
    sibling = c + 1 - 2 * core
    square = row_n == 4
    feats = x.shape[1]

    barrier = pltpu.get_barrier_semaphore()

    def greet_col(off, carry):
        pl.semaphore_signal(barrier, inc=1, device_id={"col": (c + off) % col_n})
        return carry

    def greet_row(off, carry):
        pl.semaphore_signal(barrier, inc=1, device_id={"row": (r + off) % row_n})
        return carry

    lax.fori_loop(1, col_n, greet_col, 0)
    lax.fori_loop(1, row_n, greet_row, 0)
    pl.semaphore_wait(barrier, col_n - 1 + row_n - 1)

    def a_copy(i, off):
        return pltpu.make_async_remote_copy(
            src_ref=src[i].at[(c + off) % col_n],
            dst_ref=dst[i].at[r * col_n + c],
            send_sem=a_send.at[i, off],
            recv_sem=a_recv.at[i, off],
            device_id={"col": (c + off) % col_n},
        )

    def a_start(i):
        def one(off, carry):
            a_copy(i, off).start()
            return carry

        lax.fori_loop(1, col_n, one, 0)

    def peer_of(way):
        if square:
            return (r + 1 - 2 * (r % 2)) if way == 0 else (r + 2) % 4
        return (r + 1 + way) % row_n

    ways = 2 if square else row_n - 1

    def r_copy(i, way, off, own):
        origin = (c - off + col_n) % col_n
        slot = r * col_n + origin
        return pltpu.make_async_remote_copy(
            src_ref=src[i].at[c] if own else dst[i].at[slot],
            dst_ref=dst[i].at[slot],
            send_sem=r_send.at[i, way, off],
            recv_sem=r_recv.at[i, way, off],
            device_id={"row": peer_of(way)},
        )

    def rows(i):
        for way in range(ways):
            r_copy(i, way, 0, True).start()

        def one(off, carry):
            a_copy(i, off).wait_recv()
            for way in range(ways):
                r_copy(i, way, off, False).start()
            return carry

        lax.fori_loop(1, col_n, one, 0)

    def g_copy(i, way, off):
        origin = (c - off + col_n) % col_n
        slot = peer_of(way) * col_n + origin
        half = src[i].shape[1] // 2
        part = pl.ds(way * half, half)
        return pltpu.make_async_remote_copy(
            src_ref=dst[i].at[slot, part],
            dst_ref=dst[i].at[slot, part],
            send_sem=g_send.at[i, way, off],
            recv_sem=g_recv.at[i, way, off],
            device_id={"row": peer_of(1 - way)},
        )

    def diag(i):
        def one(off, carry):
            for way in range(ways):
                r_copy(i, way, off, False).wait_recv()
                if square:
                    g_copy(i, way, off).start()
            return carry

        lax.fori_loop(0, col_n, one, 0)

    def feats_of(block, which):
        return pl.ds(pl.multiple_of((2 * block + which) * feats, feats), feats)

    def c_copy(way, t):
        block = place - t if way == 0 else place + t
        return pltpu.make_async_remote_copy(
            src_ref=x if t == 0 else whole.at[:, feats_of(block, core)],
            dst_ref=whole.at[:, feats_of(block, core)],
            send_sem=c_send.at[way, t],
            recv_sem=c_recv.at[way, t],
            device_id={"col": c + 2 if way == 0 else c - 2},
        )

    def s_copy(way, t):
        block = place - t if way == 0 else place + t
        return pltpu.make_async_remote_copy(
            src_ref=x if t == 0 else whole.at[:, feats_of(block, core)],
            dst_ref=whole.at[:, feats_of(block, core)],
            send_sem=s_send.at[way, t],
            recv_sem=s_recv.at[way, t],
            device_id={"col": sibling},
        )

    def held(way, t):
        return place >= t if way == 0 else place + t < chain

    def onward(way, t):
        return held(way, t) & ((place + 1 < chain) if way == 0 else (place >= 1))

    def step(t):
        for way in range(2):
            if t >= 1:

                @pl.when(held(way, t))
                def _(way=way):
                    c_copy(way, t - 1).wait_recv()

            if t + 1 < chain:

                @pl.when(onward(way, t))
                def _(way=way):
                    c_copy(way, t).start()

            if t >= 1 or way == 0:

                @pl.when(held(way, t))
                def _(way=way):
                    s_copy(way, t).start()

    own = [
        pltpu.make_async_copy(src[i].at[c], dst[i].at[r * col_n + c], local_sem.at[i])
        for i in range(4)
    ]
    own.append(pltpu.make_async_copy(x, whole.at[:, feats_of(place, core)], local_sem.at[4]))
    a_start(0)
    a_start(1)
    for copy in own:
        copy.start()
    rows(0)
    a_start(2)
    step(0)
    rows(1)
    diag(0)
    a_start(3)
    step(1)
    rows(2)
    diag(1)
    if chain > 2:
        step(2)
    rows(3)
    diag(2)
    for t in range(3, chain):
        step(t)
    diag(3)

    for copy in own:
        copy.wait()

    def finish(i):
        def one(off, carry):
            for way in range(ways):
                r_copy(i, way, off, False).wait_send()
                if square:
                    g_copy(i, way, off).wait()
            return carry

        def two(off, carry):
            a_copy(i, off).wait_send()
            return carry

        lax.fori_loop(0, col_n, one, 0)
        lax.fori_loop(1, col_n, two, 0)

    for i in range(4):
        finish(i)
    for t in range(chain):
        for way in range(2):
            if t + 1 < chain:

                @pl.when(onward(way, t))
                def _(way=way, t=t):
                    c_copy(way, t).wait_send()

            if t >= 1 or way == 0:

                @pl.when(held(way, t))
                def _(way=way, t=t):
                    s_copy(way, t).wait()


def move(row_n, col_n, x, *blocks):
    tok_count, feats = x.shape
    chain = col_n // 2
    ways = 2 if row_n == 4 else row_n - 1
    shapes = [jax.ShapeDtypeStruct((tok_count, col_n * feats), x.dtype)] + [
        jax.ShapeDtypeStruct((row_n * col_n,) + b.shape[1:], b.dtype) for b in blocks
    ]
    dma = pltpu.SemaphoreType.DMA
    return pl.pallas_call(
        functools.partial(move_kernel, row_n, col_n),
        out_shape=shapes,
        in_specs=[pl.BlockSpec(memory_space=pl.ANY)] * 5,
        out_specs=[pl.BlockSpec(memory_space=pl.ANY)] * 5,
        scratch_shapes=[
            dma((5,)),
            dma((4, col_n)),
            dma((4, col_n)),
            dma((4, ways, col_n)),
            dma((4, ways, col_n)),
            dma((4, 2, col_n)),
            dma((4, 2, col_n)),
            dma((2, chain)),
            dma((2, chain)),
            dma((2, chain)),
            dma((2, chain)),
        ],
        compiler_params=pltpu.CompilerParams(collective_id=0, has_side_effects=True),
    )(x, *blocks)


def on_device(
    inputs,
    norm_gain,
    query_train,
    key_train,
    value_train,
    out_train,
    adapter_down,
    adapter_up,
    lengths,
):
    cols = lax.axis_size("col")
    rows, features = query_train.shape
    heads = HEADS // cols
    width = heads * HS

    def serve(trained):
        return trained.astype(jnp.bfloat16).reshape(rows, cols, width).transpose(1, 0, 2)

    out_half = out_train.astype(jnp.bfloat16).T
    out_half = out_half.reshape(out_half.shape[0], cols, width).transpose(1, 0, 2)
    whole, *parts = move(
        lax.axis_size("row"),
        cols,
        inputs,
        serve(query_train),
        serve(key_train),
        serve(value_train),
        out_half,
    )
    parts = [part.reshape(-1, width) for part in parts]
    out_t = parts[3]

    floats = whole.astype(jnp.float32)
    mean_square = jnp.mean(floats * floats, axis=1, keepdims=True)
    normed = (floats * lax.rsqrt(mean_square + 1e-05) * norm_gain).astype(jnp.bfloat16)
    adapted = jnp.dot(normed, adapter_down, preferred_element_type=jnp.float32).astype(jnp.bfloat16)
    projected = []
    for s in range(3):
        up = adapter_up[:, s].reshape(adapter_up.shape[0], width)
        projected.append(
            (
                jnp.dot(normed, parts[s], preferred_element_type=jnp.float32)
                + jnp.dot(adapted, up, preferred_element_type=jnp.float32)
            ).astype(jnp.bfloat16)
        )
    segment = segment_of(lengths[0], normed.shape[0])
    attended = attend(*projected, segment, heads)
    partial_out = lax.dot_general(
        attended, out_t, (((1,), (1,)), ((), ())), preferred_element_type=jnp.float32
    )
    return lax.psum_scatter(
        partial_out.astype(jnp.bfloat16), "col", scatter_dimension=0, tiled=True
    )


def solution(mesh):
    in_specs = (
        P("row", "col"),
        P(),
        P(("row", "col"), None),
        P(("row", "col"), None),
        P(("row", "col"), None),
        P(None, ("row", "col")),
        P(),
        P(None, None, "col", None),
        P("row", None),
    )
    out_specs = P(("row", "col"), None)
    return jax.shard_map(
        on_device, mesh=mesh, in_specs=in_specs, out_specs=out_specs, check_vma=False
    )
```

```python
import functools
import math

import jax
import jax.numpy as jnp
from jax import lax
from jax.experimental import pallas as pl
from jax.experimental.pallas import tpu as pltpu
from jax.sharding import PartitionSpec as P

HEADS = 32
HS = 128
MOST = 512


def segment_of(lengths_row, tok_count):
    position = jnp.arange(tok_count, dtype=jnp.int32)
    order = jnp.arange(lengths_row.shape[0], dtype=jnp.int32)
    prompt_ends = jnp.sum(
        jnp.where(order[:, None] <= order[None, :], lengths_row[:, None], 0), axis=0
    )
    return jnp.sum((position[:, None] >= prompt_ends[None, :]).astype(jnp.int32), axis=1)


def tail_kernel(
    order,
    queries,
    keys,
    values,
    out_t,
    seg_col,
    seg_row,
    mixed,
    attended,
    partial,
    sib_in,
    from_low,
    from_high,
    sib_send,
    sib_recv,
    chain_send,
    low_recv,
    high_recv,
):
    c = lax.axis_index("col")
    chain = len(order)
    place, core = c // 2, c % 2
    sibling = c + 1 - 2 * core
    tok_count, width = queries.shape
    pair = tok_count // chain
    rows = pair // 2
    model = out_t.shape[0]
    step = min(512, model)
    factor = 1.0 / math.sqrt(HS)

    barrier = pltpu.get_barrier_semaphore()
    pl.semaphore_signal(barrier, inc=1, device_id={"col": sibling})

    @pl.when(place >= 1)
    def _():
        pl.semaphore_signal(barrier, inc=1, device_id={"col": c - 2})

    @pl.when(place + 1 < chain)
    def _():
        pl.semaphore_signal(barrier, inc=1, device_id={"col": c + 2})

    ends = (place == 0) | (place == chain - 1)

    @pl.when(ends)
    def _():
        pl.semaphore_wait(barrier, 2)

    @pl.when(jnp.logical_not(ends))
    def _():
        pl.semaphore_wait(barrier, 3)

    def swap(j):
        return pltpu.make_async_remote_copy(
            src_ref=partial.at[j, 1 - core],
            dst_ref=sib_in.at[j],
            send_sem=sib_send.at[j],
            recv_sem=sib_recv.at[j],
            device_id={"col": sibling},
        )

    def up(j):
        return pltpu.make_async_remote_copy(
            src_ref=partial.at[j, core],
            dst_ref=from_low.at[j],
            send_sem=chain_send.at[j],
            recv_sem=low_recv.at[j],
            device_id={"col": c + 2},
        )

    def down(j):
        return pltpu.make_async_remote_copy(
            src_ref=partial.at[j, core],
            dst_ref=from_high.at[j],
            send_sem=chain_send.at[j],
            recv_sem=high_recv.at[j],
            device_id={"col": c - 2},
        )

    def compute(j):
        first = j * pair
        end = first + pair
        low = max(0, (first - MOST + 1) // pair * pair)
        shape = (pair, end - low)
        query_pos = first + lax.broadcasted_iota(jnp.int32, shape, 0)
        key_pos = low + lax.broadcasted_iota(jnp.int32, shape, 1)
        allowed = (seg_col[first:end, :] == seg_row[:, low:end]) & (key_pos <= query_pos)

        def head(h, carry):
            lanes = pl.ds(pl.multiple_of(h * HS, HS), HS)
            scores = (
                lax.dot_general(
                    queries[first:end, lanes],
                    keys[low:end, lanes],
                    (((1,), (1,)), ((), ())),
                    preferred_element_type=jnp.float32,
                )
                * factor
            )
            scores = jnp.where(allowed, scores, -1e30)
            exponent = jnp.exp(scores - jnp.max(scores, axis=1, keepdims=True))
            inverse = 1.0 / jnp.sum(exponent, axis=1, keepdims=True)
            weights = (exponent * inverse).astype(jnp.bfloat16)
            attended[:, lanes] = jnp.dot(
                weights, values[low:end, lanes], preferred_element_type=jnp.float32
            ).astype(jnp.bfloat16)
            return carry

        lax.fori_loop(0, width // HS, head, 0)

        def piece(n, carry):
            cut = pl.ds(pl.multiple_of(n * step, step), step)
            product = lax.dot_general(
                attended[...],
                out_t[cut, :],
                (((1,), (1,)), ((), ())),
                preferred_element_type=jnp.float32,
            ).astype(jnp.bfloat16)
            partial[j, 0, :, cut] = product[:rows]
            partial[j, 1, :, cut] = product[rows:]
            return carry

        lax.fori_loop(0, model // step, piece, 0)
        swap(j).start()

    def add(j, other):
        mine = partial[j, core].astype(jnp.float32)
        partial[j, core] = (mine + other[j].astype(jnp.float32)).astype(jnp.bfloat16)

    def on_chip(j):
        swap(j).wait()
        add(j, sib_in)
        if j > 0:

            @pl.when(place == 0)
            def _():
                up(j).start()

        if j < chain - 1:

            @pl.when(place == chain - 1)
            def _():
                down(j).start()

    for index, j in enumerate(order):
        compute(j)
        if index > 0:
            on_chip(order[index - 1])
    on_chip(order[-1])

    for hop in range(1, chain - 1):
        for j in order:
            if hop < j:

                @pl.when(place == hop)
                def _(j=j):
                    up(j).wait_recv()
                    add(j, from_low)
                    up(j).start()

            if chain - 1 - hop > j:

                @pl.when(place == chain - 1 - hop)
                def _(j=j):
                    down(j).wait_recv()
                    add(j, from_high)
                    down(j).start()

    for j in range(chain):

        @pl.when(place == j)
        def _(j=j):
            total = partial[j, core].astype(jnp.float32)
            if j > 0:
                up(j).wait_recv()
                total = total + from_low[j].astype(jnp.float32)
            if j < chain - 1:
                down(j).wait_recv()
                total = total + from_high[j].astype(jnp.float32)
            mixed[...] = total.astype(jnp.bfloat16)

        @pl.when(place != j)
        def _(j=j):
            up(j).wait_send()


def tail(col_n, queries, keys, values, out_t, segment):
    tok_count = queries.shape[0]
    model, width = out_t.shape
    chain = col_n // 2
    rows = tok_count // col_n
    order = []
    for near in range((chain + 1) // 2):
        order += [chain - 1 - near] + ([near] if near != chain - 1 - near else [])
    dma = pltpu.SemaphoreType.DMA
    return pl.pallas_call(
        functools.partial(tail_kernel, tuple(order)),
        out_shape=jax.ShapeDtypeStruct((rows, model), jnp.bfloat16),
        in_specs=[pl.BlockSpec(memory_space=pltpu.VMEM)] * 6,
        out_specs=pl.BlockSpec(memory_space=pltpu.VMEM),
        scratch_shapes=[
            pltpu.VMEM((2 * rows, width), jnp.bfloat16),
            pltpu.VMEM((chain, 2, rows, model), jnp.bfloat16),
            pltpu.VMEM((chain, rows, model), jnp.bfloat16),
            pltpu.VMEM((chain, rows, model), jnp.bfloat16),
            pltpu.VMEM((chain, rows, model), jnp.bfloat16),
            dma((chain,)),
            dma((chain,)),
            dma((chain,)),
            dma((chain,)),
            dma((chain,)),
        ],
        compiler_params=pltpu.CompilerParams(
            collective_id=1, has_side_effects=True, vmem_limit_bytes=44 * 2**20
        ),
    )(queries, keys, values, out_t, segment[:, None], segment[None, :])


def move_kernel(
    row_n,
    col_n,
    x,
    w0,
    w1,
    w2,
    w3,
    whole,
    d0,
    d1,
    d2,
    d3,
    local_sem,
    a_send,
    a_recv,
    r_send,
    r_recv,
    g_send,
    g_recv,
    c_send,
    c_recv,
    s_send,
    s_recv,
):
    src, dst = (w0, w1, w2, w3), (d0, d1, d2, d3)
    r, c = lax.axis_index("row"), lax.axis_index("col")
    chain = col_n // 2
    place, core = c // 2, c % 2
    sibling = c + 1 - 2 * core
    square = row_n == 4
    feats = x.shape[1]

    barrier = pltpu.get_barrier_semaphore()

    def greet_col(off, carry):
        pl.semaphore_signal(barrier, inc=1, device_id={"col": (c + off) % col_n})
        return carry

    def greet_row(off, carry):
        pl.semaphore_signal(barrier, inc=1, device_id={"row": (r + off) % row_n})
        return carry

    lax.fori_loop(1, col_n, greet_col, 0)
    lax.fori_loop(1, row_n, greet_row, 0)
    pl.semaphore_wait(barrier, col_n - 1 + row_n - 1)

    def a_copy(i, off):
        return pltpu.make_async_remote_copy(
            src_ref=src[i].at[(c + off) % col_n],
            dst_ref=dst[i].at[r * col_n + c],
            send_sem=a_send.at[i, off],
            recv_sem=a_recv.at[i, off],
            device_id={"col": (c + off) % col_n},
        )

    def a_start(i):
        def one(off, carry):
            a_copy(i, off).start()
            return carry

        lax.fori_loop(1, col_n, one, 0)

    def peer_of(way):
        if square:
            return (r + 1 - 2 * (r % 2)) if way == 0 else (r + 2) % 4
        return (r + 1 + way) % row_n

    ways = 2 if square else row_n - 1

    def r_copy(i, way, off, own):
        origin = (c - off + col_n) % col_n
        slot = r * col_n + origin
        return pltpu.make_async_remote_copy(
            src_ref=src[i].at[c] if own else dst[i].at[slot],
            dst_ref=dst[i].at[slot],
            send_sem=r_send.at[i, way, off],
            recv_sem=r_recv.at[i, way, off],
            device_id={"row": peer_of(way)},
        )

    def rows(i):
        for way in range(ways):
            r_copy(i, way, 0, True).start()

        def one(off, carry):
            a_copy(i, off).wait_recv()
            for way in range(ways):
                r_copy(i, way, off, False).start()
            return carry

        lax.fori_loop(1, col_n, one, 0)

    def g_copy(i, way, off):
        origin = (c - off + col_n) % col_n
        slot = peer_of(way) * col_n + origin
        half = src[i].shape[1] // 2
        part = pl.ds(way * half, half)
        return pltpu.make_async_remote_copy(
            src_ref=dst[i].at[slot, part],
            dst_ref=dst[i].at[slot, part],
            send_sem=g_send.at[i, way, off],
            recv_sem=g_recv.at[i, way, off],
            device_id={"row": peer_of(1 - way)},
        )

    def diag(i):
        def one(off, carry):
            for way in range(ways):
                r_copy(i, way, off, False).wait_recv()
                if square:
                    g_copy(i, way, off).start()
            return carry

        lax.fori_loop(0, col_n, one, 0)

    def feats_of(block, which):
        return pl.ds(pl.multiple_of((2 * block + which) * feats, feats), feats)

    def c_copy(way, t):
        block = place - t if way == 0 else place + t
        return pltpu.make_async_remote_copy(
            src_ref=x if t == 0 else whole.at[:, feats_of(block, core)],
            dst_ref=whole.at[:, feats_of(block, core)],
            send_sem=c_send.at[way, t],
            recv_sem=c_recv.at[way, t],
            device_id={"col": c + 2 if way == 0 else c - 2},
        )

    def s_copy(way, t):
        block = place - t if way == 0 else place + t
        return pltpu.make_async_remote_copy(
            src_ref=x if t == 0 else whole.at[:, feats_of(block, core)],
            dst_ref=whole.at[:, feats_of(block, core)],
            send_sem=s_send.at[way, t],
            recv_sem=s_recv.at[way, t],
            device_id={"col": sibling},
        )

    def held(way, t):
        return place >= t if way == 0 else place + t < chain

    def onward(way, t):
        return held(way, t) & ((place + 1 < chain) if way == 0 else (place >= 1))

    def step(t):
        for way in range(2):
            if t >= 1:

                @pl.when(held(way, t))
                def _(way=way):
                    c_copy(way, t - 1).wait_recv()

            if t + 1 < chain:

                @pl.when(onward(way, t))
                def _(way=way):
                    c_copy(way, t).start()

            if t >= 1 or way == 0:

                @pl.when(held(way, t))
                def _(way=way):
                    s_copy(way, t).start()

    own = [
        pltpu.make_async_copy(src[i].at[c], dst[i].at[r * col_n + c], local_sem.at[i])
        for i in range(4)
    ]
    own.append(pltpu.make_async_copy(x, whole.at[:, feats_of(place, core)], local_sem.at[4]))
    a_start(0)
    a_start(1)
    for copy in own:
        copy.start()
    rows(0)
    a_start(2)
    step(0)
    rows(1)
    diag(0)
    a_start(3)
    step(1)
    rows(2)
    diag(1)
    if chain > 2:
        step(2)
    rows(3)
    diag(2)
    for t in range(3, chain):
        step(t)
    diag(3)

    for copy in own:
        copy.wait()

    def finish(i):
        def one(off, carry):
            for way in range(ways):
                r_copy(i, way, off, False).wait_send()
                if square:
                    g_copy(i, way, off).wait()
            return carry

        def two(off, carry):
            a_copy(i, off).wait_send()
            return carry

        lax.fori_loop(0, col_n, one, 0)
        lax.fori_loop(1, col_n, two, 0)

    for i in range(4):
        finish(i)
    for t in range(chain):
        for way in range(2):
            if t + 1 < chain:

                @pl.when(onward(way, t))
                def _(way=way, t=t):
                    c_copy(way, t).wait_send()

            if t >= 1 or way == 0:

                @pl.when(held(way, t))
                def _(way=way, t=t):
                    s_copy(way, t).wait()


def move(row_n, col_n, x, *blocks):
    tok_count, feats = x.shape
    chain = col_n // 2
    ways = 2 if row_n == 4 else row_n - 1
    shapes = [jax.ShapeDtypeStruct((tok_count, col_n * feats), x.dtype)] + [
        jax.ShapeDtypeStruct((row_n * col_n,) + b.shape[1:], b.dtype) for b in blocks
    ]
    dma = pltpu.SemaphoreType.DMA
    return pl.pallas_call(
        functools.partial(move_kernel, row_n, col_n),
        out_shape=shapes,
        in_specs=[pl.BlockSpec(memory_space=pl.ANY)] * 5,
        out_specs=[pl.BlockSpec(memory_space=pl.ANY)] * 5,
        scratch_shapes=[
            dma((5,)),
            dma((4, col_n)),
            dma((4, col_n)),
            dma((4, ways, col_n)),
            dma((4, ways, col_n)),
            dma((4, 2, col_n)),
            dma((4, 2, col_n)),
            dma((2, chain)),
            dma((2, chain)),
            dma((2, chain)),
            dma((2, chain)),
        ],
        compiler_params=pltpu.CompilerParams(collective_id=0, has_side_effects=True),
    )(x, *blocks)


def on_device(
    inputs,
    norm_gain,
    query_train,
    key_train,
    value_train,
    out_train,
    adapter_down,
    adapter_up,
    lengths,
):
    cols = lax.axis_size("col")
    rows, features = query_train.shape
    heads = HEADS // cols
    width = heads * HS

    def serve(trained):
        return trained.astype(jnp.bfloat16).reshape(rows, cols, width).transpose(1, 0, 2)

    out_half = out_train.astype(jnp.bfloat16).T
    out_half = out_half.reshape(out_half.shape[0], cols, width).transpose(1, 0, 2)
    whole, *parts = move(
        lax.axis_size("row"),
        cols,
        inputs,
        serve(query_train),
        serve(key_train),
        serve(value_train),
        out_half,
    )
    parts = [part.reshape(-1, width) for part in parts]
    out_t = parts[3]

    floats = whole.astype(jnp.float32)
    mean_square = jnp.mean(floats * floats, axis=1, keepdims=True)
    normed = (floats * lax.rsqrt(mean_square + 1e-05) * norm_gain).astype(jnp.bfloat16)
    adapted = jnp.dot(normed, adapter_down, preferred_element_type=jnp.float32).astype(jnp.bfloat16)
    projected = []
    for s in range(3):
        up = adapter_up[:, s].reshape(adapter_up.shape[0], width)
        projected.append(
            (
                jnp.dot(normed, parts[s], preferred_element_type=jnp.float32)
                + jnp.dot(adapted, up, preferred_element_type=jnp.float32)
            ).astype(jnp.bfloat16)
        )
    segment = segment_of(lengths[0], normed.shape[0])
    return tail(cols, *projected, out_t, segment)


def solution(mesh):
    in_specs = (
        P("row", "col"),
        P(),
        P(("row", "col"), None),
        P(("row", "col"), None),
        P(("row", "col"), None),
        P(None, ("row", "col")),
        P(),
        P(None, None, "col", None),
        P("row", None),
    )
    out_specs = P(("row", "col"), None)
    return jax.shard_map(
        on_device, mesh=mesh, in_specs=in_specs, out_specs=out_specs, check_vma=False
    )
```

```python
import functools
import math

import jax
import jax.numpy as jnp
from jax import lax
from jax.experimental import pallas as pl
from jax.experimental.pallas import tpu as pltpu
from jax.sharding import PartitionSpec as P

HEADS = 32
HS = 128
MOST = 512


def segment_of(lengths_row, tok_count):
    position = jnp.arange(tok_count, dtype=jnp.int32)
    order = jnp.arange(lengths_row.shape[0], dtype=jnp.int32)
    prompt_ends = jnp.sum(
        jnp.where(order[:, None] <= order[None, :], lengths_row[:, None], 0), axis=0
    )
    return jnp.sum((position[:, None] >= prompt_ends[None, :]).astype(jnp.int32), axis=1)


def tail_kernel(
    order,
    queries,
    keys,
    values,
    out_t,
    seg_col,
    seg_row,
    mixed,
    attended,
    partial,
    sib_in,
    from_low,
    from_high,
    sib_send,
    sib_recv,
    chain_send,
    low_recv,
    high_recv,
):
    c = lax.axis_index("col")
    chain = len(order)
    place, core = c // 2, c % 2
    sibling = c + 1 - 2 * core
    tok_count, width = queries.shape
    pair = tok_count // chain
    rows = pair // 2
    model = out_t.shape[0]
    step = min(512, model)
    factor = 1.0 / math.sqrt(HS)

    barrier = pltpu.get_barrier_semaphore()
    pl.semaphore_signal(barrier, inc=1, device_id={"col": sibling})

    @pl.when(place >= 1)
    def _():
        pl.semaphore_signal(barrier, inc=1, device_id={"col": c - 2})

    @pl.when(place + 1 < chain)
    def _():
        pl.semaphore_signal(barrier, inc=1, device_id={"col": c + 2})

    ends = (place == 0) | (place == chain - 1)

    @pl.when(ends)
    def _():
        pl.semaphore_wait(barrier, 2)

    @pl.when(jnp.logical_not(ends))
    def _():
        pl.semaphore_wait(barrier, 3)

    def swap(j):
        return pltpu.make_async_remote_copy(
            src_ref=partial.at[j, 1 - core],
            dst_ref=sib_in.at[j],
            send_sem=sib_send.at[j],
            recv_sem=sib_recv.at[j],
            device_id={"col": sibling},
        )

    def up(j):
        return pltpu.make_async_remote_copy(
            src_ref=partial.at[j, core],
            dst_ref=from_low.at[j],
            send_sem=chain_send.at[j],
            recv_sem=low_recv.at[j],
            device_id={"col": c + 2},
        )

    def down(j):
        return pltpu.make_async_remote_copy(
            src_ref=partial.at[j, core],
            dst_ref=from_high.at[j],
            send_sem=chain_send.at[j],
            recv_sem=high_recv.at[j],
            device_id={"col": c - 2},
        )

    def compute(j):
        first = j * pair
        end = first + pair
        low = max(0, (first - MOST + 1) // pair * pair)
        shape = (pair, end - low)
        query_pos = first + lax.broadcasted_iota(jnp.int32, shape, 0)
        key_pos = low + lax.broadcasted_iota(jnp.int32, shape, 1)
        allowed = (seg_col[first:end, :] == seg_row[:, low:end]) & (key_pos <= query_pos)

        def head(h, carry):
            lanes = pl.ds(pl.multiple_of(h * HS, HS), HS)
            scores = (
                lax.dot_general(
                    queries[first:end, lanes],
                    keys[low:end, lanes],
                    (((1,), (1,)), ((), ())),
                    preferred_element_type=jnp.float32,
                )
                * factor
            )
            scores = jnp.where(allowed, scores, -1e30)
            exponent = jnp.exp(scores - jnp.max(scores, axis=1, keepdims=True))
            inverse = 1.0 / jnp.sum(exponent, axis=1, keepdims=True)
            weights = (exponent * inverse).astype(jnp.bfloat16)
            attended[:, lanes] = jnp.dot(
                weights, values[low:end, lanes], preferred_element_type=jnp.float32
            ).astype(jnp.bfloat16)
            return carry

        lax.fori_loop(0, width // HS, head, 0)

        def piece(n, carry):
            cut = pl.ds(pl.multiple_of(n * step, step), step)
            product = lax.dot_general(
                attended[...],
                out_t[cut, :],
                (((1,), (1,)), ((), ())),
                preferred_element_type=jnp.float32,
            ).astype(jnp.bfloat16)
            partial[j, 0, :, cut] = product[:rows]
            partial[j, 1, :, cut] = product[rows:]
            return carry

        lax.fori_loop(0, model // step, piece, 0)
        swap(j).start()

    def add(j, other):
        mine = partial[j, core].astype(jnp.float32)
        partial[j, core] = (mine + other[j].astype(jnp.float32)).astype(jnp.bfloat16)

    def on_chip(j):
        swap(j).wait()
        add(j, sib_in)
        if j > 0:

            @pl.when(place == 0)
            def _():
                up(j).start()

        if j < chain - 1:

            @pl.when(place == chain - 1)
            def _():
                down(j).start()

    for index, j in enumerate(order):
        compute(j)
        if index > 0:
            on_chip(order[index - 1])
    on_chip(order[-1])

    for hop in range(1, chain - 1):
        for j in order:
            if hop < j:

                @pl.when(place == hop)
                def _(j=j):
                    up(j).wait_recv()
                    add(j, from_low)
                    up(j).start()

            if chain - 1 - hop > j:

                @pl.when(place == chain - 1 - hop)
                def _(j=j):
                    down(j).wait_recv()
                    add(j, from_high)
                    down(j).start()

    for j in range(chain):

        @pl.when(place == j)
        def _(j=j):
            total = partial[j, core].astype(jnp.float32)
            if j > 0:
                up(j).wait_recv()
                total = total + from_low[j].astype(jnp.float32)
            if j < chain - 1:
                down(j).wait_recv()
                total = total + from_high[j].astype(jnp.float32)
            mixed[...] = total.astype(jnp.bfloat16)

        @pl.when(place != j)
        def _(j=j):
            up(j).wait_send()


def tail(col_n, queries, keys, values, out_t, segment):
    tok_count = queries.shape[0]
    model, width = out_t.shape
    chain = col_n // 2
    rows = tok_count // col_n
    order = []
    for near in range((chain + 1) // 2):
        order += [chain - 1 - near] + ([near] if near != chain - 1 - near else [])
    dma = pltpu.SemaphoreType.DMA
    return pl.pallas_call(
        functools.partial(tail_kernel, tuple(order)),
        out_shape=jax.ShapeDtypeStruct((rows, model), jnp.bfloat16),
        in_specs=[pl.BlockSpec(memory_space=pltpu.VMEM)] * 6,
        out_specs=pl.BlockSpec(memory_space=pltpu.VMEM),
        scratch_shapes=[
            pltpu.VMEM((2 * rows, width), jnp.bfloat16),
            pltpu.VMEM((chain, 2, rows, model), jnp.bfloat16),
            pltpu.VMEM((chain, rows, model), jnp.bfloat16),
            pltpu.VMEM((chain, rows, model), jnp.bfloat16),
            pltpu.VMEM((chain, rows, model), jnp.bfloat16),
            dma((chain,)),
            dma((chain,)),
            dma((chain,)),
            dma((chain,)),
            dma((chain,)),
        ],
        compiler_params=pltpu.CompilerParams(
            collective_id=1, has_side_effects=True, vmem_limit_bytes=44 * 2**20
        ),
    )(queries, keys, values, out_t, segment[:, None], segment[None, :])


def move_kernel(
    row_n,
    col_n,
    x,
    w0,
    w1,
    w2,
    w3,
    squares,
    whole,
    d0,
    d1,
    d2,
    d3,
    all_squares,
    h0,
    h1,
    h2,
    t_send,
    t_recv,
    local_sem,
    a_send,
    a_recv,
    r_send,
    r_recv,
    g_send,
    g_recv,
    c_send,
    c_recv,
    s_send,
    s_recv,
):
    wide, src, dst = (w0, w1, w2), (h0, h1, h2, w3), (d0, d1, d2, d3)
    r, c = lax.axis_index("row"), lax.axis_index("col")
    chain = col_n // 2
    place, core = c // 2, c % 2
    sibling = c + 1 - 2 * core
    square = row_n == 4
    feats = x.shape[1]

    def cast(i):
        width = src[i].shape[2]

        def one(peer, carry):
            lanes = pl.ds(pl.multiple_of(peer * width, width), width)
            src[i][peer] = wide[i][:, lanes].astype(jnp.bfloat16)
            return carry

        lax.fori_loop(0, col_n, one, 0)

    barrier = pltpu.get_barrier_semaphore()

    def greet_col(off, carry):
        pl.semaphore_signal(barrier, inc=1, device_id={"col": (c + off) % col_n})
        return carry

    def greet_row(off, carry):
        pl.semaphore_signal(barrier, inc=1, device_id={"row": (r + off) % row_n})
        return carry

    lax.fori_loop(1, col_n, greet_col, 0)
    lax.fori_loop(1, row_n, greet_row, 0)
    cast(0)
    pl.semaphore_wait(barrier, col_n - 1 + row_n - 1)

    def a_copy(i, off):
        return pltpu.make_async_remote_copy(
            src_ref=src[i].at[(c + off) % col_n],
            dst_ref=dst[i].at[r * col_n + c],
            send_sem=a_send.at[i, off],
            recv_sem=a_recv.at[i, off],
            device_id={"col": (c + off) % col_n},
        )

    def t_copy(off):
        return pltpu.make_async_remote_copy(
            src_ref=squares,
            dst_ref=all_squares.at[c],
            send_sem=t_send.at[off],
            recv_sem=t_recv.at[off],
            device_id={"col": (c + off) % col_n},
        )

    def t_start(off, carry):
        t_copy(off).start()
        return carry

    def t_wait(off, carry):
        t_copy(off).wait()
        return carry

    def a_start(i):
        def one(off, carry):
            a_copy(i, off).start()
            return carry

        lax.fori_loop(1, col_n, one, 0)

    def peer_of(way):
        if square:
            return (r + 1 - 2 * (r % 2)) if way == 0 else (r + 2) % 4
        return (r + 1 + way) % row_n

    ways = 2 if square else row_n - 1

    def r_copy(i, way, off, own):
        origin = (c - off + col_n) % col_n
        slot = r * col_n + origin
        return pltpu.make_async_remote_copy(
            src_ref=src[i].at[c] if own else dst[i].at[slot],
            dst_ref=dst[i].at[slot],
            send_sem=r_send.at[i, way, off],
            recv_sem=r_recv.at[i, way, off],
            device_id={"row": peer_of(way)},
        )

    def rows(i):
        for way in range(ways):
            r_copy(i, way, 0, True).start()

        def one(off, carry):
            a_copy(i, off).wait_recv()
            for way in range(ways):
                r_copy(i, way, off, False).start()
            return carry

        lax.fori_loop(1, col_n, one, 0)

    def g_copy(i, way, off):
        origin = (c - off + col_n) % col_n
        slot = peer_of(way) * col_n + origin
        half = src[i].shape[1] // 2
        part = pl.ds(way * half, half)
        return pltpu.make_async_remote_copy(
            src_ref=dst[i].at[slot, part],
            dst_ref=dst[i].at[slot, part],
            send_sem=g_send.at[i, way, off],
            recv_sem=g_recv.at[i, way, off],
            device_id={"row": peer_of(1 - way)},
        )

    def diag(i):
        def one(off, carry):
            for way in range(ways):
                r_copy(i, way, off, False).wait_recv()
                if square:
                    g_copy(i, way, off).start()
            return carry

        lax.fori_loop(0, col_n, one, 0)

    def feats_of(block, which):
        return pl.ds(pl.multiple_of((2 * block + which) * feats, feats), feats)

    def c_copy(way, t):
        block = place - t if way == 0 else place + t
        return pltpu.make_async_remote_copy(
            src_ref=x if t == 0 else whole.at[:, feats_of(block, core)],
            dst_ref=whole.at[:, feats_of(block, core)],
            send_sem=c_send.at[way, t],
            recv_sem=c_recv.at[way, t],
            device_id={"col": c + 2 if way == 0 else c - 2},
        )

    def s_copy(way, t):
        block = place - t if way == 0 else place + t
        return pltpu.make_async_remote_copy(
            src_ref=x if t == 0 else whole.at[:, feats_of(block, core)],
            dst_ref=whole.at[:, feats_of(block, core)],
            send_sem=s_send.at[way, t],
            recv_sem=s_recv.at[way, t],
            device_id={"col": sibling},
        )

    def held(way, t):
        return place >= t if way == 0 else place + t < chain

    def onward(way, t):
        return held(way, t) & ((place + 1 < chain) if way == 0 else (place >= 1))

    def step(t):
        for way in range(2):
            if t >= 1:

                @pl.when(held(way, t))
                def _(way=way):
                    c_copy(way, t - 1).wait_recv()

            if t + 1 < chain:

                @pl.when(onward(way, t))
                def _(way=way):
                    c_copy(way, t).start()

            if t >= 1 or way == 0:

                @pl.when(held(way, t))
                def _(way=way):
                    s_copy(way, t).start()

    own = [
        pltpu.make_async_copy(src[i].at[c], dst[i].at[r * col_n + c], local_sem.at[i])
        for i in range(4)
    ]
    own.append(pltpu.make_async_copy(x, whole.at[:, feats_of(place, core)], local_sem.at[4]))
    own.append(pltpu.make_async_copy(squares, all_squares.at[c], local_sem.at[5]))
    a_start(0)
    cast(1)
    a_start(1)
    cast(2)
    lax.fori_loop(1, col_n, t_start, 0)
    for copy in own:
        copy.start()
    rows(0)
    a_start(2)
    step(0)
    rows(1)
    diag(0)
    a_start(3)
    step(1)
    rows(2)
    diag(1)
    if chain > 2:
        step(2)
    rows(3)
    diag(2)
    for t in range(3, chain):
        step(t)
    diag(3)

    for copy in own:
        copy.wait()

    def finish(i):
        def one(off, carry):
            for way in range(ways):
                r_copy(i, way, off, False).wait_send()
                if square:
                    g_copy(i, way, off).wait()
            return carry

        def two(off, carry):
            a_copy(i, off).wait_send()
            return carry

        lax.fori_loop(0, col_n, one, 0)
        lax.fori_loop(1, col_n, two, 0)

    lax.fori_loop(1, col_n, t_wait, 0)
    for i in range(4):
        finish(i)
    for t in range(chain):
        for way in range(2):
            if t + 1 < chain:

                @pl.when(onward(way, t))
                def _(way=way, t=t):
                    c_copy(way, t).wait_send()

            if t >= 1 or way == 0:

                @pl.when(held(way, t))
                def _(way=way, t=t):
                    s_copy(way, t).wait()


def move(row_n, col_n, x, wide, out_half, squares):
    tok_count, feats = x.shape
    chain = col_n // 2
    ways = 2 if row_n == 4 else row_n - 1
    rows = wide[0].shape[0]
    width = wide[0].shape[1] // col_n
    blocks = [jax.ShapeDtypeStruct((col_n, rows, width), jnp.bfloat16)] * 3 + [out_half]
    shapes = [jax.ShapeDtypeStruct((tok_count, col_n * feats), x.dtype)] + [
        jax.ShapeDtypeStruct((row_n * col_n,) + b.shape[1:], b.dtype) for b in blocks
    ]
    shapes.append(jax.ShapeDtypeStruct((col_n,) + squares.shape, squares.dtype))
    dma = pltpu.SemaphoreType.DMA
    return pl.pallas_call(
        functools.partial(move_kernel, row_n, col_n),
        out_shape=shapes,
        in_specs=[pl.BlockSpec(memory_space=pl.ANY)]
        + [pl.BlockSpec(memory_space=pltpu.VMEM)] * 3
        + [pl.BlockSpec(memory_space=pl.ANY)] * 2,
        out_specs=[pl.BlockSpec(memory_space=pl.ANY)] * 6,
        scratch_shapes=[pltpu.VMEM((col_n, rows, width), jnp.bfloat16)] * 3
        + [
            dma((col_n,)),
            dma((col_n,)),
            dma((6,)),
            dma((4, col_n)),
            dma((4, col_n)),
            dma((4, ways, col_n)),
            dma((4, ways, col_n)),
            dma((4, 2, col_n)),
            dma((4, 2, col_n)),
            dma((2, chain)),
            dma((2, chain)),
            dma((2, chain)),
            dma((2, chain)),
        ],
        compiler_params=pltpu.CompilerParams(
            collective_id=0, has_side_effects=True, vmem_limit_bytes=32 * 2**20
        ),
    )(x, *wide, out_half, squares)


def on_device(
    inputs,
    norm_gain,
    query_train,
    key_train,
    value_train,
    out_train,
    adapter_down,
    adapter_up,
    lengths,
):
    cols = lax.axis_size("col")
    rows, features = query_train.shape
    heads = HEADS // cols
    width = heads * HS

    tok_count, feats = inputs.shape
    out_half = out_train.astype(jnp.bfloat16).T
    out_half = out_half.reshape(out_half.shape[0], cols, width).transpose(1, 0, 2)
    floats = inputs.astype(jnp.float32)
    squares = jnp.sum(floats * floats, axis=1).reshape(tok_count // HS, HS)
    gain = lax.dynamic_slice_in_dim(norm_gain, lax.axis_index("col") * feats, feats, 0)
    gained = (floats * gain).astype(jnp.bfloat16)
    whole, *parts, all_squares = move(
        lax.axis_size("row"),
        cols,
        gained,
        (query_train, key_train, value_train),
        out_half,
        squares,
    )
    parts = [part.reshape(-1, width) for part in parts]
    out_t = parts[3]

    mean_square = jnp.sum(all_squares, axis=0).reshape(tok_count, 1) / (cols * feats)
    inverse = lax.rsqrt(mean_square + 1e-05)
    adapted = (
        jnp.dot(whole, adapter_down, preferred_element_type=jnp.float32) * inverse
    ).astype(jnp.bfloat16)
    projected = []
    for s in range(3):
        up = adapter_up[:, s].reshape(adapter_up.shape[0], width)
        projected.append(
            (
                jnp.dot(whole, parts[s], preferred_element_type=jnp.float32) * inverse
                + jnp.dot(adapted, up, preferred_element_type=jnp.float32)
            ).astype(jnp.bfloat16)
        )
    segment = segment_of(lengths[0], tok_count)
    return tail(cols, *projected, out_t, segment)


def solution(mesh):
    in_specs = (
        P("row", "col"),
        P(),
        P(("row", "col"), None),
        P(("row", "col"), None),
        P(("row", "col"), None),
        P(None, ("row", "col")),
        P(),
        P(None, None, "col", None),
        P("row", None),
    )
    out_specs = P(("row", "col"), None)
    return jax.shard_map(
        on_device, mesh=mesh, in_specs=in_specs, out_specs=out_specs, check_vma=False
    )
```
